32 devices in a mesh: row: 8 (over y, x, core), col: 4 (over z).
Axes of the slice: x: 2, y: 2, z: 4, core: 2. Of those that a mesh axis runs over, the one named last changes fastest.
Arguments:
- coeffs: bfloat16 [8192, 2048], P('row', 'col'), may hold values from -1.5 to 1.5
- basis_values: bfloat16 [32, 512, 512], P(('row', 'col')), may hold values from -1 to 1
- point_weights: float32 [32, 512], P(('row', 'col')), may hold values from 0.05 to 1
- point_counts: int32 [32], P(('row', 'col')), may hold values from 1 to 512, as said below
- func_lists: int32 [32, 512], P(('row', 'col')), may hold values from 0 to 8191, as said below
Outputs:
- density: bfloat16 [8192, 8192], P('col', 'row')
- potential: float32 [8192, 8192], P('col', 'row')
The draws below stay inside these ranges and needn't reach their ends.
Inputs may be any that keep to these rules, and one draw needn't show every extreme that they name: `func_lists`: A batch held by device index d of row+col has its functions in the three row-axis blocks (d // 4 - 1) mod 8, d // 4 and its successor, each block 1024 functions, indices taken modulo 8192; a list holds distinct indices. `point_counts`: some batch has all 512 points live in every draw.
All inputs are finite; a program needn't handle non-finite values.
Results may differ from the reference program's by a relative error of at most 0.006.
Values may be sent and summed in bfloat16 or wider, within the bound.
No kernel may reach another device: no remote copies, remote signals or barrier semaphores. Data moves between devices by JAX's collectives and lax.ppermute only.
A program may use at most 128 MiB of HBM per device.

```python
import math
import jax
import jax.numpy as jnp
from jax import lax

NBF = 8192
NOCC = 2048
NLIST = 512
NPTS = 512
BATCH_DEV = 1
NBATCH = 32
TILE = 1024
WIN = 3072
N_ROW = 8
N_COL = 4


group_count = 8


common_gain = 2.8284271


def draw_point_counts(key, part):
    first_key, second_key = jax.random.split(key)
    levels = jax.random.randint(first_key, (NBATCH,), 1, NPTS + 1)
    position = jax.random.randint(second_key, (), 0, NBATCH)
    return levels.at[position].set(NPTS).astype(jnp.int32)


def draw_func_lists(key, part):
    keys_all = jax.random.split(key, NBATCH)

    def one_list(batch_key):
        picked = jax.random.permutation(batch_key, WIN - 3)[:NLIST - 3]
        mapped = jnp.where(picked + 1 < TILE - 1, picked + 1, picked + 2)
        fixed_ends = jnp.array([0, TILE - 1, WIN - 1], jnp.int32)
        return jnp.sort(jnp.concatenate([fixed_ends, mapped.astype(jnp.int32)]))
    offsets = jax.vmap(one_list)(keys_all)
    holder_row = jnp.arange(NBATCH, dtype=jnp.int32) // BATCH_DEV // N_COL
    first_func = (holder_row - 1) % N_ROW * TILE
    return ((first_func[:, None] + offsets) % NBF).astype(jnp.int32)


def draw_coeffs(key, part):
    common_key = jax.random.fold_in(key, 0)
    single_key = jax.random.fold_in(key, 1)
    group_key = jax.random.fold_in(key, 3)
    factor = (2.0 * NOCC) ** (-0.5)
    lead_orbitals = NOCC // 4
    groups = jax.random.randint(group_key, (NBF,), 0, group_count)
    orbital_gain = (jnp.arange(NOCC) < lead_orbitals).astype(jnp.float32) * common_gain
    common = jnp.clip(jax.random.normal(common_key, (group_count, NOCC), jnp.float32), -2.5, 2.5)
    single = jnp.clip(jax.random.normal(single_key, (NBF, NOCC), jnp.float32), -2.5, 2.5)
    values = jnp.take(common, groups, axis=0) * orbital_gain[None, :] + single
    return (factor * values).astype(jnp.bfloat16)


def draw_basis_values(key, part):
    noise_key, shared_key = jax.random.split(key, 2)
    spread = (2.0 * NLIST) ** (-0.5)
    shared_weight = (3.0 / NLIST) ** 0.5
    noise = jnp.clip(jax.random.normal(noise_key, (NBATCH, NPTS, NLIST), jnp.float32), -4.0, 4.0)
    shared = jnp.clip(jax.random.normal(shared_key, (NBATCH, NPTS, 1), jnp.float32), -3.0, 3.0)
    values = noise + shared_weight * shared
    return (spread * values).astype(jnp.bfloat16)


def block_levels(stream_key, dims, shards, low, largest):
    def one(axis_at, shards_of):
        steps = jax.random.uniform(jax.random.fold_in(jax.random.fold_in(stream_key, 6), axis_at), (shards_of,), jnp.float32, low / len(shards), largest / len(shards))
        return jnp.repeat(jnp.exp(steps), dims[axis_at] // shards_of).reshape((-1,) + (1,) * (len(dims) - axis_at - 1))

    gain = one(*shards[0])
    for cut in shards[1:]:
        gain = gain * one(*cut)
    return gain


def setup_inputs(seed: int = 0) -> dict:
    keys = jax.random.split(jax.random.key(seed), 6)
    coeffs = draw_coeffs(jax.random.fold_in(keys[5], 71), 0)
    basis_values = draw_basis_values(jax.random.fold_in(keys[5], 71), 0)
    point_weights = jnp.clip(jnp.exp(math.log(1.0) - 2.9957323 * jax.random.uniform(keys[2], (NBATCH, NPTS), jnp.float32) ** block_levels(keys[2], (NBATCH, NPTS), ((0, 32),), -0.2, 0.2)), 0.05, 1.0)
    point_counts = draw_point_counts(jax.random.fold_in(keys[5], 71), 0)
    func_lists = draw_func_lists(jax.random.fold_in(keys[5], 71), 0)
    return {"coeffs": coeffs, "basis_values": basis_values, "point_weights": point_weights, "point_counts": point_counts, "func_lists": func_lists}


slater_coef = 0.9847450218426965


def exchange_potential(density_pts):
    return -slater_coef * jnp.power(density_pts + 1.0, 1.0 / 3.0)


def reference(coeffs, basis_values, point_weights, point_counts, func_lists):
    density = (2.0 * jnp.dot(coeffs, coeffs.T, preferred_element_type=jnp.float32)).astype(jnp.bfloat16)

    def add_batch(summed, batch_item):
        basis_block, weights, count_pts, func_index = batch_item
        dens_block = density[func_index][:, func_index]
        projected = jnp.dot(basis_block, dens_block, preferred_element_type=jnp.float32)
        density_pts = jnp.sum(projected * basis_block.astype(jnp.float32), axis=1)
        is_live = jnp.arange(NPTS) < count_pts
        pot_pts = jnp.where(is_live, weights * exchange_potential(density_pts), jnp.float32(0.0))
        scaled = (basis_block.astype(jnp.float32) * pot_pts[:, None]).astype(jnp.bfloat16)
        pot_block = jnp.dot(basis_block.T, scaled, preferred_element_type=jnp.float32)
        return summed.at[func_index[:, None], func_index[None, :]].add(pot_block), None

    potential, _ = lax.scan(add_batch, jnp.zeros((NBF, NBF), jnp.float32), (basis_values, point_weights, point_counts, func_lists))
    return density, potential
```

```python
import functools

import jax
import jax.numpy as jnp
from jax import lax
from jax.experimental import pallas as pl
from jax.experimental.pallas import tpu as pltpu
from jax.sharding import PartitionSpec as P

slater_coef = 0.9847450218426965
both = ("row", "col")
extra = 16
lanes = 128
vmem_bytes = 52 * 1024 * 1024


def latin(a, b, n):
    if n & (n - 1) == 0:
        return a ^ b
    return (b - a + n) % n


def ring(x, n, by=1):
    return lax.ppermute(x, "col", [(i, (i + by) % n) for i in range(n)])


def row_shift(x, n, by):
    return lax.ppermute(x, "row", [(i, (i + by) % n) for i in range(n)])


def as_column(row_vec, width=lanes):
    return jnp.broadcast_to(row_vec, (width, row_vec.shape[1])).T


def list_of(b_ref, npts):
    hi = b_ref[npts : npts + 1, :].astype(jnp.float32)
    lo = b_ref[npts + 1 : npts + 2, :].astype(jnp.float32)
    return hi * 128.0 + lo


def weight_of(b_ref, npts):
    w1 = b_ref[npts + 2 : npts + 3, :].astype(jnp.float32)
    w2 = b_ref[npts + 3 : npts + 4, :].astype(jnp.float32)
    w3 = b_ref[npts + 4 : npts + 5, :].astype(jnp.float32)
    return (w1 + w2) + w3


def one_hot_columns(column, base, width, out_ref):
    for at in range(0, width, lanes):
        spot = lax.broadcasted_iota(jnp.int32, column.shape, 1) + (base + at)
        out_ref[:, at : at + lanes] = jnp.where(column == spot, 1.0, 0.0).astype(jnp.bfloat16)


def rho_kernel(n_col, n_row, npts, where_ref, *refs):
    b_refs, (c_before, c_own, c_after, out_ref, pick_ref) = refs[:n_col], refs[n_col:]
    tile = c_own.shape[0]
    total = tile * n_row
    row, col = where_ref[0], where_ref[1]
    start = lax.rem(row + n_row - 1, n_row) * tile
    for k, b_ref in enumerate(b_refs):
        index = list_of(b_ref, npts).astype(jnp.int32) - start
        index = jnp.where(index < 0, index + total, index)
        one_hot_columns(as_column(index), 0, 3 * tile, pick_ref)
        picked = jnp.zeros((index.shape[1], c_own.shape[1]), jnp.float32)
        for t, c_ref in enumerate((c_before, c_own, c_after)):
            picked += jnp.dot(
                pick_ref[:, t * tile : (t + 1) * tile], c_ref[...], preferred_element_type=jnp.float32
            )
        orbitals = jnp.dot(
            b_ref[:npts, :], picked.astype(jnp.bfloat16), preferred_element_type=jnp.float32
        )
        rho = 2.0 * jnp.sum(orbitals * orbitals, axis=1, keepdims=True)
        rho = jnp.broadcast_to(rho, (npts, lanes)).T[0:1, :]
        out_ref[pl.ds(lax.rem(col + n_col - k, n_col), 1), :] = rho


def potential_kernel(n_col, n_row, npts, where_ref, *refs):
    b_own = refs[:n_col]
    b_prev, b_next, rho_own, rho_prev, rho_next, out_ref, x_ref, list_ref, pick_ref = refs[n_col:]
    nlist = b_prev.shape[2]
    tile = out_ref.shape[1]
    blocks = out_ref.shape[0] // tile
    chunk = min(256, tile)
    row, col = where_ref[0], where_ref[1]
    out_ref[...] = jnp.zeros_like(out_ref)
    for shift, batches, rho_ref in (
        (0, b_own, rho_own),
        (-1, [b_prev.at[k] for k in range(n_col)], rho_prev),
        (1, [b_next.at[k] for k in range(n_col)], rho_next),
    ):
        source = lax.rem(row + n_row + shift, n_row)
        for k, b_ref in enumerate(batches):
            rho = rho_ref[pl.ds(lax.rem(col + n_col - k, n_col), 1), :]
            pot = weight_of(b_ref, npts) * (-slater_coef * jnp.exp(jnp.log(rho + 1.0) * (1.0 / 3.0)))
            pot_col = as_column(pot)
            basis = b_ref[:npts, :]
            pot_full = jnp.concatenate([pot_col] * (nlist // lanes), axis=1)
            scaled = (basis.astype(jnp.float32) * pot_full).astype(jnp.bfloat16)
            vblock = lax.dot_general(
                basis, scaled, (((0,), (0,)), ((), ())), preferred_element_type=jnp.float32
            ).astype(jnp.bfloat16)
            index = list_of(b_ref, npts).astype(jnp.int32)
            list_ref[:, k * nlist : (k + 1) * nlist] = jnp.broadcast_to(index, (8, nlist))
            one_hot_columns(as_column(index), row * tile, tile, pick_ref)
            x_ref[k * nlist : (k + 1) * nlist, :] = jnp.dot(
                vblock, pick_ref[...], preferred_element_type=jnp.float32
            ).astype(jnp.bfloat16)
        for s in range(blocks):
            block = col * blocks + s
            inside = lax.rem(block - source + 1 + 2 * n_row, n_row) < 3

            @pl.when(inside)
            def _(block=block, s=s):
                def add(step, carry):
                    spot = lax.broadcasted_iota(jnp.int32, (chunk, list_ref.shape[1]), 0) + (
                        block * tile + step * chunk
                    )
                    place = jnp.where(list_ref[0:1, :] == spot, 1.0, 0.0).astype(jnp.bfloat16)
                    rows = pl.ds(pl.multiple_of(s * tile + step * chunk, chunk), chunk)
                    out_ref[rows, :] += jnp.dot(
                        place, x_ref[...], preferred_element_type=jnp.float32
                    )
                    return carry

                lax.fori_loop(0, tile // chunk, add, 0)


def density_kernel(n_col, where_ref, panel_ref, *refs):
    own_refs, out_ref = refs[:n_col], refs[n_col]
    col = where_ref[1]
    total = None
    for k, own_ref in enumerate(own_refs):
        group = latin(col, lax.rem(col + n_col - k, n_col), n_col)
        part = lax.dot_general(
            panel_ref[group], own_ref[...], (((1,), (1,)), ((), ())), preferred_element_type=jnp.float32
        )
        total = part if total is None else total + part
    out_ref[...] = (2.0 * total).astype(out_ref.dtype)


def on_device(coeffs, basis_values, point_weights, point_counts, func_lists):
    n_row, n_col = lax.axis_size("row"), lax.axis_size("col")
    tile, width = coeffs.shape
    blocks = n_row // n_col
    npts, nlist = basis_values.shape[1:]
    row, col = lax.axis_index("row"), lax.axis_index("col")
    where = jnp.stack([row, col]).astype(jnp.int32)

    def device(r, c):
        return r * n_col + c

    live = jnp.arange(npts, dtype=jnp.int32) < point_counts[0]
    weights = jnp.where(live, point_weights[0], 0.0)
    w1 = weights.astype(jnp.bfloat16)
    rest = weights - w1.astype(jnp.float32)
    w2 = rest.astype(jnp.bfloat16)
    w3 = (rest - w2.astype(jnp.float32)).astype(jnp.bfloat16)
    lists = func_lists[0]
    tail = jnp.stack([(lists // 128).astype(jnp.bfloat16), (lists % 128).astype(jnp.bfloat16), w1, w2, w3])
    tail = jnp.pad(tail, ((0, extra - tail.shape[0]), (0, 0)))
    batch = jnp.concatenate([basis_values[0], tail], axis=0)

    batches = [batch]
    for _ in range(1, n_col):
        batches.append(ring(batches[-1], n_col))
    before = row_shift(coeffs, n_row, 1)
    after = row_shift(coeffs, n_row, -1)

    spread = []
    for r in range(n_row):
        for c in range(n_col):
            spread.append((device(r, c), device(latin(r // blocks, c, n_col) * blocks + r % blocks, c)))
    piece = lax.ppermute(coeffs, both, spread)
    lift = []
    for r in range(n_row):
        for c in range(n_col):
            lift.append((device(r, c), device(r, latin(r // blocks, c, n_col))))
    piece = lax.ppermute(piece, both, lift)
    panel = lax.all_gather(piece, "row", axis=0, tiled=True)
    panel = panel.reshape(n_col, blocks * tile, width)

    def neighbours(x, by):
        pairs = []
        for r in range(n_row):
            for c in range(n_col):
                source = (r + by) % n_row
                if any((c * blocks + s - source + 1) % n_row < 3 for s in range(blocks)):
                    pairs.append((device(source, c), device(r, c)))
        return lax.ppermute(x, both, pairs)

    row_batches = jnp.stack(batches)
    prev_batches = neighbours(row_batches, -1)
    next_batches = neighbours(row_batches, 1)

    own = [coeffs]
    for _ in range(1, n_col):
        own.append(ring(own[-1], n_col))

    smem = pl.BlockSpec(memory_space=pltpu.SMEM)
    vmem = pl.BlockSpec(memory_space=pltpu.VMEM)
    partial = pl.pallas_call(
        functools.partial(rho_kernel, n_col, n_row, npts),
        out_shape=jax.ShapeDtypeStruct((n_col, npts), jnp.float32),
        in_specs=[smem] + [vmem] * (n_col + 3),
        out_specs=vmem,
        scratch_shapes=[pltpu.VMEM((nlist, 3 * tile), jnp.bfloat16)],
        compiler_params=pltpu.CompilerParams(vmem_limit_bytes=vmem_bytes),
        cost_estimate=pl.CostEstimate(
            flops=2 * n_col * nlist * width * (3 * tile + npts), bytes_accessed=6 << 20, transcendentals=0
        ),
        name="rho_partial",
    )(where, *batches, before, coeffs, after)
    rho = lax.psum(partial, "col")
    rho_prev = row_shift(rho, n_row, 1)
    rho_next = row_shift(rho, n_row, -1)

    potential = pl.pallas_call(
        functools.partial(potential_kernel, n_col, n_row, npts),
        out_shape=jax.ShapeDtypeStruct((blocks * tile, tile), jnp.float32),
        in_specs=[smem] + [vmem] * (n_col + 5),
        out_specs=vmem,
        scratch_shapes=[
            pltpu.VMEM((n_col * nlist, tile), jnp.bfloat16),
            pltpu.VMEM((8, n_col * nlist), jnp.int32),
            pltpu.VMEM((nlist, tile), jnp.bfloat16),
        ],
        compiler_params=pltpu.CompilerParams(vmem_limit_bytes=vmem_bytes),
        cost_estimate=pl.CostEstimate(
            flops=6 * n_col * nlist * (nlist * npts + nlist * tile + blocks * tile * tile),
            bytes_accessed=16 << 20,
            transcendentals=0,
        ),
        name="potential",
    )(where, *batches, prev_batches, next_batches, rho, rho_prev, rho_next)

    chunk = min(256, tile)
    density = pl.pallas_call(
        functools.partial(density_kernel, n_col),
        out_shape=jax.ShapeDtypeStruct((blocks * tile, tile), jnp.bfloat16),
        grid_spec=pltpu.PrefetchScalarGridSpec(
            num_scalar_prefetch=1,
            grid=(blocks * tile // chunk,),
            in_specs=[pl.BlockSpec((n_col, chunk, width), lambda i, where: (0, i, 0))]
            + [pl.BlockSpec((tile, width), lambda i, where: (0, 0))] * n_col,
            out_specs=pl.BlockSpec((chunk, tile), lambda i, where: (i, 0)),
        ),
        compiler_params=pltpu.CompilerParams(vmem_limit_bytes=vmem_bytes),
        cost_estimate=pl.CostEstimate(
            flops=2 * blocks * tile * tile * width * n_col, bytes_accessed=16 << 20, transcendentals=0
        ),
        name="density",
    )(where, panel, *own)
    return density, potential


def solution(mesh):
    in_specs = (
        P("row", "col"),
        P(("row", "col"), None, None),
        P(("row", "col"), None),
        P(("row", "col")),
        P(("row", "col"), None),
    )
    out_specs = (P("col", "row"), P("col", "row"))
    return jax.shard_map(
        on_device, mesh=mesh, in_specs=in_specs, out_specs=out_specs, check_vma=False
    )
```

```python
import functools

import jax
import jax.numpy as jnp
from jax import lax
from jax.experimental import pallas as pl
from jax.experimental.pallas import tpu as pltpu
from jax.sharding import PartitionSpec as P

slater_coef = 0.9847450218426965
both = ("row", "col")
extra = 16
lanes = 128
vmem_bytes = 52 * 1024 * 1024


def after(x, *done):
    return lax.optimization_barrier((x,) + done)[0]


def ring(x, n, by=1):
    return lax.ppermute(x, "col", [(i, (i + by) % n) for i in range(n)])


def row_shift(x, n, by):
    return lax.ppermute(x, "row", [(i, (i + by) % n) for i in range(n)])


def as_column(row_vec, width=lanes):
    return jnp.broadcast_to(row_vec, (width, row_vec.shape[1])).T


def list_of(b_ref, npts):
    hi = b_ref[npts : npts + 1, :].astype(jnp.float32)
    lo = b_ref[npts + 1 : npts + 2, :].astype(jnp.float32)
    return hi * 128.0 + lo


def weight_of(b_ref, npts):
    w1 = b_ref[npts + 2 : npts + 3, :].astype(jnp.float32)
    w2 = b_ref[npts + 3 : npts + 4, :].astype(jnp.float32)
    w3 = b_ref[npts + 4 : npts + 5, :].astype(jnp.float32)
    return (w1 + w2) + w3


def one_hot_columns(column, base, width, out_ref):
    for at in range(0, width, lanes):
        spot = lax.broadcasted_iota(jnp.int32, column.shape, 1) + (base + at)
        out_ref[:, at : at + lanes] = jnp.where(column == spot, 1.0, 0.0).astype(jnp.bfloat16)


def rho_kernel(n_col, n_row, npts, where_ref, *refs):
    b_refs, (c_before, c_own, c_after, out_ref, pick_ref) = refs[:n_col], refs[n_col:]
    tile = c_own.shape[0]
    total = tile * n_row
    row, col = where_ref[0], where_ref[1]
    start = lax.rem(row + n_row - 1, n_row) * tile
    for k, b_ref in enumerate(b_refs):
        index = list_of(b_ref, npts).astype(jnp.int32) - start
        index = jnp.where(index < 0, index + total, index)
        one_hot_columns(as_column(index), 0, 3 * tile, pick_ref)
        picked = jnp.zeros((index.shape[1], c_own.shape[1]), jnp.float32)
        for t, c_ref in enumerate((c_before, c_own, c_after)):
            picked += jnp.dot(
                pick_ref[:, t * tile : (t + 1) * tile], c_ref[...], preferred_element_type=jnp.float32
            )
        orbitals = jnp.dot(
            b_ref[:npts, :], picked.astype(jnp.bfloat16), preferred_element_type=jnp.float32
        )
        rho = 2.0 * jnp.sum(orbitals * orbitals, axis=1, keepdims=True)
        rho = jnp.broadcast_to(rho, (npts, lanes)).T[0:1, :]
        out_ref[pl.ds(lax.rem(col + n_col - k, n_col), 1), :] = rho


def touches(block, source, n_row):
    return lax.rem(block - source + 1 + 2 * n_row, n_row) < 3


def columns_kernel(n_col, n_row, npts, shift, where_ref, b_ref, rho_ref, x_ref, list_ref, pick_ref):
    nlist = b_ref.shape[2]
    tile = x_ref.shape[1]
    blocks = n_row // n_col
    row, col = where_ref[0], where_ref[1]
    source = lax.rem(row + n_row + shift, n_row)
    used = touches(col * blocks, source, n_row)
    for s in range(1, blocks):
        used = jnp.logical_or(used, touches(col * blocks + s, source, n_row))

    @pl.when(used)
    def _():
        for k in range(n_col):
            rho = rho_ref[pl.ds(lax.rem(col + n_col - k, n_col), 1), :]
            weight = weight_of(b_ref.at[k], npts)
            pot = weight * (-slater_coef * jnp.exp(jnp.log(rho + 1.0) * (1.0 / 3.0)))
            pot_full = jnp.concatenate([as_column(pot)] * (nlist // lanes), axis=1)
            basis = b_ref[k, :npts, :]
            scaled = (basis.astype(jnp.float32) * pot_full).astype(jnp.bfloat16)
            vblock = lax.dot_general(
                basis, scaled, (((0,), (0,)), ((), ())), preferred_element_type=jnp.float32
            ).astype(jnp.bfloat16)
            index = list_of(b_ref.at[k], npts).astype(jnp.int32)
            list_ref[:, k * nlist : (k + 1) * nlist] = jnp.broadcast_to(index, (8, nlist))
            one_hot_columns(as_column(index), row * tile, tile, pick_ref)
            x_ref[k * nlist : (k + 1) * nlist, :] = jnp.dot(
                vblock, pick_ref[...], preferred_element_type=jnp.float32
            ).astype(jnp.bfloat16)


def rows_kernel(n_col, n_row, tile, where_ref, *refs):
    x_refs, list_refs, out_ref = refs[:3], refs[3:6], refs[6]
    blocks = n_row // n_col
    chunk = out_ref.shape[0]
    row, col = where_ref[0], where_ref[1]
    base = col * blocks * tile + pl.program_id(0) * chunk
    block = lax.div(base, tile)
    out_ref[...] = jnp.zeros_like(out_ref)
    for shift, x_ref, list_ref in zip((0, -1, 1), x_refs, list_refs):
        source = lax.rem(row + n_row + shift, n_row)

        @pl.when(touches(block, source, n_row))
        def _(x_ref=x_ref, list_ref=list_ref):
            spot = lax.broadcasted_iota(jnp.int32, (chunk, list_ref.shape[1]), 0) + base
            place = jnp.where(list_ref[0:1, :] == spot, 1.0, 0.0).astype(jnp.bfloat16)
            out_ref[...] += jnp.dot(place, x_ref[...], preferred_element_type=jnp.float32)


def density_kernel(n_col, where_ref, first_ref, rest_ref, *refs):
    own_refs, out_ref = refs[:n_col], refs[n_col]
    parts, _, rows, _ = rest_ref.shape
    for p in range(parts):
        at = slice(p * rows, (p + 1) * rows)
        total = None
        for k, own_ref in enumerate(own_refs):
            panel = first_ref[at, :] if k == 0 else rest_ref[p, k - 1]
            part = lax.dot_general(
                panel, own_ref[...], (((1,), (1,)), ((), ())), preferred_element_type=jnp.float32
            )
            total = part if total is None else total + part
        out_ref[at, :] = (2.0 * total).astype(out_ref.dtype)


def on_device(coeffs, basis_values, point_weights, point_counts, func_lists):
    n_row, n_col = lax.axis_size("row"), lax.axis_size("col")
    tile, width = coeffs.shape
    blocks = n_row // n_col
    npts, nlist = basis_values.shape[1:]
    row, col = lax.axis_index("row"), lax.axis_index("col")
    where = jnp.stack([row, col]).astype(jnp.int32)

    def device(r, c):
        return r * n_col + c

    live = jnp.arange(npts, dtype=jnp.int32) < point_counts[0]
    weights = jnp.where(live, point_weights[0], 0.0)
    w1 = weights.astype(jnp.bfloat16)
    rest = weights - w1.astype(jnp.float32)
    w2 = rest.astype(jnp.bfloat16)
    w3 = (rest - w2.astype(jnp.float32)).astype(jnp.bfloat16)
    index = func_lists[0]
    tail = jnp.stack([(index // 128).astype(jnp.bfloat16), (index % 128).astype(jnp.bfloat16), w1, w2, w3])
    tail = jnp.pad(tail, ((0, extra - tail.shape[0]), (0, 0)))
    batch = jnp.concatenate([basis_values[0], tail], axis=0)

    slice_all = lax.all_gather(coeffs, "row", axis=0, tiled=True)

    batches = [batch]
    for _ in range(1, n_col):
        batches.append(ring(batches[-1], n_col))

    own = [coeffs, ring(after(coeffs, batches[-1]), n_col)]

    def neighbours(x, by):
        pairs = []
        for r in range(n_row):
            for c in range(n_col):
                source = (r + by) % n_row
                if any((c * blocks + s - source + 1) % n_row < 3 for s in range(blocks)):
                    pairs.append((device(source, c), device(r, c)))
        return lax.ppermute(x, both, pairs)

    row_batches = after(jnp.stack(batches), slice_all)
    prev_batches = neighbours(row_batches, -1)
    next_batches = neighbours(row_batches, 1)

    smem = pl.BlockSpec(memory_space=pltpu.SMEM)
    vmem = pl.BlockSpec(memory_space=pltpu.VMEM)
    def blocks_of(shift):
        return pl.BlockSpec((tile, width), lambda i, where: (lax.rem(where[0] + n_row + shift, n_row), 0))

    def whole(*shape):
        return pl.BlockSpec(shape, lambda i, where: (0,) * len(shape))

    partial = pl.pallas_call(
        functools.partial(rho_kernel, n_col, n_row, npts),
        out_shape=jax.ShapeDtypeStruct((n_col, npts), jnp.float32),
        grid_spec=pltpu.PrefetchScalarGridSpec(
            num_scalar_prefetch=1,
            grid=(1,),
            in_specs=[whole(npts + extra, nlist)] * n_col + [blocks_of(-1), blocks_of(0), blocks_of(1)],
            out_specs=whole(n_col, npts),
            scratch_shapes=[pltpu.VMEM((nlist, 3 * tile), jnp.bfloat16)],
        ),
        compiler_params=pltpu.CompilerParams(vmem_limit_bytes=vmem_bytes),
        cost_estimate=pl.CostEstimate(
            flops=2 * n_col * nlist * width * (3 * tile + npts), bytes_accessed=6 << 20, transcendentals=0
        ),
        name="rho_partial",
    )(where, *batches, slice_all, slice_all, slice_all)
    rho = lax.psum(partial, "col")
    part = blocks * tile // n_row
    parts = []
    slices = after(slice_all, rho, own[1])
    for k in range(1, n_col):
        start = lax.rem(col + k, n_col) * (blocks * tile) + row * part
        parts.append(ring(lax.dynamic_slice_in_dim(slices, start, part, 0), n_col, k))
    panel = lax.all_gather(after(jnp.stack(parts), prev_batches, next_batches), "row", axis=0)

    rho_prev = row_shift(rho, n_row, 1)
    rho_next = row_shift(rho, n_row, -1)

    placed, lists = [], []
    for shift, batches_of, rho_of in (
        (0, row_batches, rho),
        (-1, prev_batches, rho_prev),
        (1, next_batches, rho_next),
    ):
        x, index = pl.pallas_call(
            functools.partial(columns_kernel, n_col, n_row, npts, shift),
            out_shape=[
                jax.ShapeDtypeStruct((n_col * nlist, tile), jnp.bfloat16),
                jax.ShapeDtypeStruct((8, n_col * nlist), jnp.int32),
            ],
            in_specs=[smem, vmem, vmem],
            out_specs=[vmem, vmem],
            scratch_shapes=[pltpu.VMEM((nlist, tile), jnp.bfloat16)],
            compiler_params=pltpu.CompilerParams(vmem_limit_bytes=vmem_bytes),
            cost_estimate=pl.CostEstimate(
                flops=2 * n_col * nlist * nlist * (npts + tile), bytes_accessed=6 << 20, transcendentals=0
            ),
            name="columns",
        )(where, batches_of, rho_of)
        placed.append(x)
        lists.append(index)
        if shift == 0:
            own.append(ring(after(own[-1], rho), n_col))
    for _ in range(3, n_col):
        own.append(ring(after(own[-1], placed[0], rho_prev, rho_next), n_col))

    chunk = min(256, tile)
    potential = pl.pallas_call(
        functools.partial(rows_kernel, n_col, n_row, tile),
        out_shape=jax.ShapeDtypeStruct((blocks * tile, tile), jnp.float32),
        grid_spec=pltpu.PrefetchScalarGridSpec(
            num_scalar_prefetch=1,
            grid=(blocks * tile // chunk,),
            in_specs=[whole(n_col * nlist, tile)] * 3 + [whole(8, n_col * nlist)] * 3,
            out_specs=pl.BlockSpec((chunk, tile), lambda i, where: (i, 0)),
        ),
        compiler_params=pltpu.CompilerParams(vmem_limit_bytes=vmem_bytes),
        cost_estimate=pl.CostEstimate(
            flops=5 * n_col * nlist * blocks * tile * tile, bytes_accessed=20 << 20, transcendentals=0
        ),
        name="rows",
    )(where, *placed, *lists)

    step = max(chunk // part, 1)
    density = pl.pallas_call(
        functools.partial(density_kernel, n_col),
        out_shape=jax.ShapeDtypeStruct((blocks * tile, tile), jnp.bfloat16),
        grid_spec=pltpu.PrefetchScalarGridSpec(
            num_scalar_prefetch=1,
            grid=(n_row // step,),
            in_specs=[
                pl.BlockSpec((step * part, width), lambda i, where: (where[1] * (n_row // step) + i, 0)),
                pl.BlockSpec((step, n_col - 1, part, width), lambda i, where: (i, 0, 0, 0)),
            ]
            + [whole(tile, width)] * n_col,
            out_specs=pl.BlockSpec((step * part, tile), lambda i, where: (i, 0)),
        ),
        compiler_params=pltpu.CompilerParams(vmem_limit_bytes=vmem_bytes),
        cost_estimate=pl.CostEstimate(
            flops=2 * blocks * tile * tile * width * n_col, bytes_accessed=16 << 20, transcendentals=0
        ),
        name="density",
    )(where, slice_all, panel, *own)
    return density, potential


def solution(mesh):
    in_specs = (
        P("row", "col"),
        P(("row", "col"), None, None),
        P(("row", "col"), None),
        P(("row", "col")),
        P(("row", "col"), None),
    )
    out_specs = (P("col", "row"), P("col", "row"))
    return jax.shard_map(
        on_device, mesh=mesh, in_specs=in_specs, out_specs=out_specs, check_vma=False
    )
```
